32 devices in a mesh: pix: 16 (over z, y, x), tm: 2 (over core).
Axes of the slice: x: 2, y: 2, z: 4, core: 2. Of those that a mesh axis runs over, the one named last changes fastest.
Arguments:
- movie: bfloat16 [32768, 512], P('pix', 'tm'), may hold values from -6 to 6
- traces: bfloat16 [512, 512], P('pix', 'tm'), may hold values from 0 to 2
- footprints: bfloat16 [4096, 128], P('pix'), may hold values from 0 to 0.2
- slot_block: int32 [4096], P('pix'), may hold values from 0 to 15
- slot_neuron: int32 [4096], P('pix'), may hold values from 0 to 31
- bucket_fill: int32 [16, 16], P('pix'), may hold values from 1 to 16, as said below
Outputs:
- traces_new: bfloat16 [512, 512], P('pix', 'tm')
- footprints_new: float32 [4096, 128], P('pix')
The draws below stay inside these ranges and needn't reach their ends.
Inputs may be any that keep to these rules, and one draw needn't show every extreme that they name: `bucket_fill`: A tile has at most 16 used slots for one owner; in every draw some owner gets 16 from every tile, and every tile fills 16 for some owner.
All inputs are finite; a program needn't handle non-finite values.
Results may differ from the reference program's by a relative error of at most 0.0049.
Values may be sent and summed in bfloat16 or wider, within the bound.
A program may use at most 64 MiB of HBM per device.

```python
import jax
import jax.numpy as jnp
from jax import lax

BLOCK = 128
NB_DEV = 16
SLOT_DEV = 256
NEUR_DEV = 32
PIX_DEV = 2048
PIXELS = 32768
FRAMES = 512
NEURONS = 512
CAP = 16
N_PIX = 16


def draw_bucket_fill(key, part):
    key_high, key_raw, key_col, key_dest = jax.random.split(key, 4)
    highest = jax.random.randint(key_high, (1, N_PIX), 2, 2 * CAP + 1)
    raw_fill = jax.random.randint(key_raw, (N_PIX, N_PIX), 1, highest)
    counts = jnp.minimum(raw_fill, CAP)
    columns = jnp.arange(N_PIX, dtype=jnp.int32)[None, :]
    forced_col = jax.random.randint(key_col, (N_PIX, 1), 0, N_PIX)
    counts = jnp.where(columns == forced_col, CAP, counts)
    full_dest = jax.random.randint(key_dest, (), 0, N_PIX)
    counts = jnp.where(columns == full_dest, CAP, counts)
    return counts.astype(jnp.int32)


def draw_footprints(key, part):
    key_keep, key_value = jax.random.split(jax.random.fold_in(key, 7))
    row_total = N_PIX * SLOT_DEV
    support = jax.random.randint(key_keep, (row_total, BLOCK), 0, 4 * SLOT_DEV) < 3 * NB_DEV
    values = jax.random.uniform(key_value, (row_total, BLOCK), jnp.float32, 0.0, 0.199)
    return jnp.where(support, values, 0.0).astype(jnp.bfloat16)


def set_ends(values, rng, low, top_value):
    dims = values.shape
    spot = [jax.random.randint(jax.random.fold_in(rng, axis), (), 0, dims[axis]) for axis in range(len(dims))]
    values = values.at[tuple(spot)].set(low)
    longest = dims.index(max(dims))
    spot[longest] = (spot[longest] + 1) % dims[longest]
    return values.at[tuple(spot)].set(top_value)


def levels(key, dims, cuts, low, high):
    def one(dim, shards_of):
        heights = jax.random.uniform(jax.random.fold_in(jax.random.fold_in(key, 6), dim), (shards_of,), jnp.float32, low / len(cuts), high / len(cuts))
        return jnp.repeat(jnp.exp(heights), dims[dim] // shards_of).reshape((-1,) + (1,) * (len(dims) - dim - 1))

    factor_of = one(*cuts[0])
    for cut in cuts[1:]:
        factor_of = factor_of * one(*cut)
    return factor_of


def normal_values(stream_key, extent, scale, most, cuts=(), kind=jnp.bfloat16):
    drawn = jax.random.normal(stream_key, extent, jnp.float32) * scale
    if len(cuts) > 0:
        drawn = levels(stream_key, extent, cuts, -0.22, 0.18) * drawn
    return jnp.clip(drawn, min=-most, max=most).astype(kind)


def setup_inputs(seed: int = 0) -> dict:
    splits = jax.random.split(jax.random.key(seed), 7)
    return {
        "movie": normal_values(splits[0], (PIXELS, FRAMES), 1.0, 6.0, ((0, 16), (1, 2))),
        "traces": jnp.clip(2.0 * jax.random.uniform(splits[1], (NEURONS, FRAMES), jnp.float32) ** levels(splits[1], (NEURONS, FRAMES), ((0, 16), (1, 2)), -0.2, 0.2), 0.0, 2.0).astype(jnp.bfloat16),
        "footprints": draw_footprints(jax.random.fold_in(splits[6], 71), 0),
        "slot_block": set_ends(jax.random.randint(splits[3], (N_PIX * SLOT_DEV,), 0, NB_DEV), jax.random.fold_in(splits[3], 1), 0, NB_DEV - 1).astype(jnp.int32),
        "slot_neuron": set_ends(jax.random.randint(splits[4], (N_PIX * SLOT_DEV,), 0, NEUR_DEV), jax.random.fold_in(splits[4], 1), 0, NEUR_DEV - 1).astype(jnp.int32),
        "bucket_fill": draw_bucket_fill(jax.random.fold_in(splits[6], 71), 0),
    }


def prepare_tile(foot, blocks, fill_row, bucket_of, position):
    usable = position < fill_row[bucket_of]
    masked = foot * usable[:, None].astype(jnp.bfloat16)
    block_pick = blocks[:, None] == jnp.arange(NB_DEV, dtype=jnp.int32)[None, :]
    dense_map = (block_pick.astype(jnp.bfloat16)[:, :, None] * masked[:, None, :]).reshape(SLOT_DEV, PIX_DEV)
    return usable, masked, block_pick, dense_map


def reference(movie, traces, footprints, slot_block, slot_neuron, bucket_fill):
    capacity = SLOT_DEV // N_PIX
    slot_index = jnp.arange(SLOT_DEV, dtype=jnp.int32)
    bucket_of = (slot_index // capacity).astype(jnp.int32)
    position = (slot_index % capacity).astype(jnp.int32)
    movie_tiles = movie.reshape(N_PIX, PIX_DEV, FRAMES)
    foot_tiles = footprints.reshape(N_PIX, SLOT_DEV, BLOCK)
    block_tiles = slot_block.reshape(N_PIX, SLOT_DEV)
    neuron_tiles = slot_neuron.reshape(N_PIX, SLOT_DEV)

    def first_pass(carry, tile):
        summed, power = carry
        pixels, foot, blocks, neurons, fill_row = tile
        usable, masked, block_pick, dense_map = prepare_tile(foot, blocks, fill_row, bucket_of, position)
        global_row = (bucket_of * NEUR_DEV + neurons).astype(jnp.int32)
        slot_traces = traces[global_row]
        rebuilt = jnp.dot(dense_map.T, slot_traces, preferred_element_type=jnp.float32)
        residual = (pixels.astype(jnp.float32) - rebuilt).astype(jnp.bfloat16)
        projection = jnp.dot(dense_map, residual, preferred_element_type=jnp.float32)
        slot_power = jnp.sum(masked.astype(jnp.float32) ** 2, axis=1)
        summed = summed.at[global_row].add(projection)
        power = power.at[global_row].add(slot_power)
        return (summed, power), None

    start = (jnp.zeros((NEURONS, FRAMES), jnp.float32), jnp.zeros((NEURONS,), jnp.float32))
    (summed, power), _ = lax.scan(first_pass, start, (movie_tiles, foot_tiles, block_tiles, neuron_tiles, bucket_fill))
    updated = jnp.maximum(0.0, traces.astype(jnp.float32) + summed / jnp.maximum(power, 0.5)[:, None]).astype(jnp.bfloat16)

    def second_pass(tile):
        pixels, foot, blocks, neurons, fill_row = tile
        usable, masked, block_pick, dense_map = prepare_tile(foot, blocks, fill_row, bucket_of, position)
        global_row = (bucket_of * NEUR_DEV + neurons).astype(jnp.int32)
        slot_traces = updated[global_row]
        rebuilt = jnp.dot(dense_map.T, slot_traces, preferred_element_type=jnp.float32)
        residual = (pixels.astype(jnp.float32) - rebuilt).astype(jnp.bfloat16)
        products = jnp.dot(residual, slot_traces.T, preferred_element_type=jnp.float32)
        numerator = jnp.einsum("bps,sb->sp", products.reshape(NB_DEV, BLOCK, SLOT_DEV), block_pick.astype(jnp.float32), precision=lax.Precision.HIGHEST)
        trace_power = jnp.sum(slot_traces.astype(jnp.float32) ** 2, axis=1)
        grown = jnp.maximum(0.0, masked.astype(jnp.float32) + numerator / (trace_power + 1e-6)[:, None])
        return jnp.where(usable[:, None], grown, 0.0)

    new_foot = lax.map(second_pass, (movie_tiles, foot_tiles, block_tiles, neuron_tiles, bucket_fill))
    return updated, new_foot.reshape(N_PIX * SLOT_DEV, BLOCK)
```

```python
import functools

import jax
import jax.numpy as jnp
from jax import lax
from jax.experimental import pallas as pl
from jax.experimental.pallas import tpu as pltpu
from jax.sharding import PartitionSpec as P

BLOCK = 128
ROWS = 16
SIDE = 128
F32 = jnp.float32
BF16 = jnp.bfloat16
NN = (((1,), (0,)), ((), ()))
NT = (((1,), (1,)), ((), ()))
TN = (((0,), (0,)), ((), ()))


def dot(a, b, dims=NN):
    return lax.dot_general(a, b, dims, preferred_element_type=F32)


def split(value):
    high = value.astype(BF16)
    return high, (value - high.astype(F32)).astype(BF16)


def iota(shape, dim):
    return lax.broadcasted_iota(jnp.int32, shape, dim)


def near_order(n):
    return sorted(range(1, n), key=lambda k: (abs(k - n // 2), k))


def kernel(
    n, t, movie_hbm, traces_hbm, foot_hbm, block_hbm, neuron_hbm, fill_hbm,
    new_ref, grown_ref,
    movie, foot, block_ref, neuron_ref, fill_ref,
    all_traces, proj_out, proj_in, back_out, back_in, num_out, num_in, pow_out, pow_in,
    local_sem, send_sem, recv_sem, tm_send, tm_recv,
):
    me = lax.axis_index("pix")
    core = lax.axis_index("tm")
    slots = foot.shape[0]
    cap = slots // n
    neur = traces_hbm.shape[0]
    frames = movie.shape[1]
    blocks = movie.shape[0] // BLOCK
    neurons = n * neur

    def pix_id(peer):
        return (peer, core)

    def peers(body):
        if n <= 16:
            for k in near_order(n):
                body(lax.rem(me + k, n))
        else:
            lax.fori_loop(1, n, lambda k, _: (body(lax.rem(me + k, n)), 0)[1], 0)

    def part(index, size):
        return pl.ds(pl.multiple_of(index * size, size), size)

    barrier = pltpu.get_barrier_semaphore()
    peers(lambda p: pl.semaphore_signal(barrier, inc=1, device_id=pix_id(p)))
    for k in range(1, t):
        pl.semaphore_signal(barrier, inc=1, device_id=(me, lax.rem(core + k, t)))

    mine = all_traces.at[part(me, neur)]
    loads = [
        pltpu.make_async_copy(a, b, local_sem.at[i])
        for i, (a, b) in enumerate(
            [
                (traces_hbm, mine),
                (foot_hbm, foot),
                (block_hbm, block_ref),
                (neuron_hbm, neuron_ref),
                (fill_hbm, fill_ref),
                (movie_hbm, movie),
            ]
        )
    ]
    for load in loads:
        load.start()
    loads[0].wait()
    pl.semaphore_wait(barrier, n - 1 + t - 1)

    def trace_copy(p, source):
        return pltpu.make_async_remote_copy(
            src_ref=mine,
            dst_ref=all_traces.at[part(source, neur)],
            send_sem=send_sem.at[0, p],
            recv_sem=recv_sem.at[0, source],
            device_id=pix_id(p),
        )

    peers(lambda p: trace_copy(p, me).start())
    for load in loads[1:5]:
        load.wait()

    diag = iota((slots, slots), 0) == iota((slots, slots), 1)

    def column(row):
        return jnp.sum(jnp.where(diag, row.astype(F32), 0.0), axis=1, keepdims=True)

    block_row = block_ref[...].astype(F32)
    block_col = column(block_row)
    neuron_col = column(neuron_ref[...])
    owner_hit = lax.div(iota((slots, n), 0), cap) == iota((slots, n), 1)
    fill_col = jnp.sum(jnp.where(owner_hit, fill_ref[...].astype(F32), 0.0), axis=1, keepdims=True)
    row_of = iota((slots, 1), 0)
    usable = lax.rem(row_of, cap).astype(F32) < fill_col
    masked = jnp.where(usable, foot[...].astype(F32), 0.0)
    masked_b = masked.astype(BF16)
    same_block = block_col == block_row
    power = jnp.sum(masked * masked, axis=1, keepdims=True)
    lane = iota((slots, SIDE), 1)
    power_high, rest = split(power)
    power_mid, power_low = split(power - power_high.astype(F32))
    side = jnp.where(
        lane == 0,
        neuron_col,
        jnp.where(
            lane == 1,
            power_high.astype(F32),
            jnp.where(
                lane == 2,
                power_mid.astype(F32),
                jnp.where(lane == 3, power_low.astype(F32), 0.0),
            ),
        ),
    ).astype(BF16)

    padded = n * ROWS
    if cap == ROWS:
        widen = narrow = lambda x: x
    else:
        slot_row = lax.div(iota((padded, slots), 0), ROWS) * cap + lax.rem(
            iota((padded, slots), 0), ROWS
        )
        real = lax.rem(iota((padded, slots), 0), ROWS) < cap
        place = ((slot_row == iota((padded, slots), 1)) & real).astype(BF16)

        def widen(x):
            return dot(place, x).astype(BF16)

        def narrow(x):
            return dot(place, x, TN).astype(BF16)

    proj_out[:, frames:] = widen(side)

    gram = jnp.where(same_block, dot(masked_b, masked_b, NT), 0.0)
    neuron_id = lax.div(row_of, cap).astype(F32) * neur + neuron_col
    pick = (neuron_id == iota((slots, neurons), 1).astype(F32)).astype(BF16)
    gram_high, gram_low = split(gram)
    couple_high, couple_low = split(dot(gram_high, pick) + dot(gram_low, pick))

    loads[5].wait()
    base = jnp.zeros((slots, frames), F32)
    for b in range(0, blocks, 2):
        pair = jnp.concatenate(
            [jnp.where(block_col == float(b + j), masked, 0.0).astype(BF16) for j in range(2)],
            axis=1,
        )
        base += dot(pair, movie[b * BLOCK : (b + 2) * BLOCK, :])

    peers(lambda p: trace_copy(p, p).wait_recv())
    gathered = all_traces[...]
    projection = base - (dot(couple_high, gathered) + dot(couple_low, gathered))
    proj_out[:, :frames] = widen(projection.astype(BF16))

    def proj_copy(p, source):
        return pltpu.make_async_remote_copy(
            src_ref=proj_out.at[part(p, ROWS)],
            dst_ref=proj_in.at[part(source, ROWS)],
            send_sem=send_sem.at[1, p],
            recv_sem=recv_sem.at[1, source],
            device_id=pix_id(p),
        )

    peers(lambda p: proj_copy(p, me).start())
    proj_in[part(me, ROWS), :] = proj_out[part(me, ROWS), :]
    peers(lambda p: proj_copy(p, p).wait_recv())

    got = proj_in[...]
    asked = got[:, frames : frames + 1].astype(F32)
    owner_pick = asked == iota((padded, neur), 1).astype(F32)
    if cap != ROWS:
        owner_pick &= lax.rem(iota((padded, neur), 0), ROWS) < cap
    owner_pick = owner_pick.astype(F32).astype(BF16)
    sums = dot(owner_pick, got, TN)
    total_power = (
        sums[:, frames + 1 : frames + 2]
        + sums[:, frames + 2 : frames + 3]
        + sums[:, frames + 3 : frames + 4]
    )
    own = all_traces[part(me, neur), :].astype(F32)
    updated = jnp.maximum(0.0, own + sums[:, :frames] / jnp.maximum(total_power, 0.5)).astype(BF16)
    new_ref[...] = updated
    back_out[...] = dot(owner_pick, updated).astype(BF16)

    def back_copy(p, source):
        return pltpu.make_async_remote_copy(
            src_ref=back_out.at[part(p, ROWS)],
            dst_ref=back_in.at[part(source, ROWS)],
            send_sem=send_sem.at[2, p],
            recv_sem=recv_sem.at[2, source],
            device_id=pix_id(p),
        )

    peers(lambda p: back_copy(p, me).start())
    back_in[part(me, ROWS), :] = back_out[part(me, ROWS), :]
    peers(lambda p: back_copy(p, p).wait_recv())

    fresh = narrow(back_in[...])
    fresh_f = fresh.astype(F32)
    pow_out[...] = jnp.broadcast_to(
        jnp.sum(fresh_f * fresh_f, axis=1, keepdims=True), (slots, BLOCK)
    )

    def tm_copy(index, out, into, q, source):
        return pltpu.make_async_remote_copy(
            src_ref=out,
            dst_ref=into.at[source],
            send_sem=tm_send.at[index, q],
            recv_sem=tm_recv.at[index, source],
            device_id=(me, q),
        )

    partners = [lax.rem(core + k, t) for k in range(1, t)]
    for q in partners:
        tm_copy(0, pow_out, pow_in, q, core).start()
    overlap = jnp.where(same_block, dot(fresh, fresh, NT), 0.0)
    over_high, over_low = split(overlap)
    numerator = -(dot(over_high, masked_b) + dot(over_low, masked_b))
    for b in range(0, blocks, 2):
        product = dot(fresh, movie[b * BLOCK : (b + 2) * BLOCK, :], NT)
        for j in range(2):
            numerator += jnp.where(
                block_col == float(b + j), product[:, j * BLOCK : (j + 1) * BLOCK], 0.0
            )
    num_out[...] = numerator
    for q in partners:
        tm_copy(1, num_out, num_in, q, core).start()
    pow_in[core] = pow_out[...]
    num_in[core] = numerator
    for q in partners:
        tm_copy(0, pow_out, pow_in, q, q).wait_recv()
        tm_copy(1, num_out, num_in, q, q).wait_recv()
    num_all, pow_all = num_in[0], pow_in[0]
    for q in range(1, t):
        num_all += num_in[q]
        pow_all += pow_in[q]
    grown = jnp.maximum(0.0, masked + num_all / (pow_all + 1e-06))
    grown_ref[...] = jnp.where(usable, grown, 0.0)

    peers(lambda p: trace_copy(p, me).wait_send())
    peers(lambda p: proj_copy(p, me).wait_send())
    peers(lambda p: back_copy(p, me).wait_send())
    for q in partners:
        tm_copy(0, pow_out, pow_in, q, core).wait_send()
        tm_copy(1, num_out, num_in, q, core).wait_send()


def local(n, t, movie, traces, footprints, slot_block, slot_neuron, bucket_fill):
    slots = footprints.shape[0]
    neur, frames = traces.shape
    padded = n * ROWS
    return pl.pallas_call(
        functools.partial(kernel, n, t),
        out_shape=(
            jax.ShapeDtypeStruct((neur, frames), BF16),
            jax.ShapeDtypeStruct((slots, BLOCK), F32),
        ),
        in_specs=[pl.BlockSpec(memory_space=pl.ANY)] * 6,
        out_specs=[pl.BlockSpec(memory_space=pltpu.VMEM)] * 2,
        scratch_shapes=[
            pltpu.VMEM(movie.shape, BF16),
            pltpu.VMEM(footprints.shape, BF16),
            pltpu.VMEM((1, slots), jnp.int32),
            pltpu.VMEM((1, slots), jnp.int32),
            pltpu.VMEM((1, n), jnp.int32),
            pltpu.VMEM((n * neur, frames), BF16),
            pltpu.VMEM((padded, frames + SIDE), BF16),
            pltpu.VMEM((padded, frames + SIDE), BF16),
            pltpu.VMEM((padded, frames), BF16),
            pltpu.VMEM((padded, frames), BF16),
            pltpu.VMEM((slots, BLOCK), F32),
            pltpu.VMEM((t, slots, BLOCK), F32),
            pltpu.VMEM((slots, BLOCK), F32),
            pltpu.VMEM((t, slots, BLOCK), F32),
            pltpu.SemaphoreType.DMA((6,)),
            pltpu.SemaphoreType.DMA((3, n)),
            pltpu.SemaphoreType.DMA((3, n)),
            pltpu.SemaphoreType.DMA((2, t)),
            pltpu.SemaphoreType.DMA((2, t)),
        ],
        compiler_params=pltpu.CompilerParams(
            collective_id=0, has_side_effects=True, vmem_limit_bytes=48 * 1024 * 1024
        ),
    )(
        movie,
        traces,
        footprints,
        slot_block.reshape(1, slots),
        slot_neuron.reshape(1, slots),
        bucket_fill,
    )


def solution(mesh):
    return jax.shard_map(
        functools.partial(local, mesh.shape["pix"], mesh.shape["tm"]),
        mesh=mesh,
        in_specs=(
            P("pix", "tm"),
            P("pix", "tm"),
            P("pix", None),
            P("pix"),
            P("pix"),
            P("pix", None),
        ),
        out_specs=(P("pix", "tm"), P("pix", None)),
        check_vma=False,
    )
```

```python
import functools

import jax
import jax.numpy as jnp
from jax import lax
from jax.experimental import pallas as pl
from jax.experimental.pallas import tpu as pltpu
from jax.sharding import PartitionSpec as P

BLOCK = 128
ROWS = 16
LANES = 128
PARTS = 1
F32 = jnp.float32
BF16 = jnp.bfloat16
NN = (((1,), (0,)), ((), ()))
NT = (((1,), (1,)), ((), ()))
TN = (((0,), (0,)), ((), ()))


def dot(a, b, dims=NN):
    return lax.dot_general(a, b, dims, preferred_element_type=F32)


def split(value):
    high = value.astype(BF16)
    return high, (value - high.astype(F32)).astype(BF16)


def exact_dot(ones, b):
    high, rest = b.astype(BF16), b - b.astype(BF16).astype(F32)
    mid, low = split(rest)
    return dot(ones, high) + dot(ones, mid) + dot(ones, low)


def iota(shape, dim):
    return lax.broadcasted_iota(jnp.int32, shape, dim)


def near_order(n):
    return sorted(range(1, n), key=lambda k: (abs(k - n // 2), k))


def kernel(
    n, t, movie_hbm, traces_hbm, foot_hbm, block_hbm, neuron_hbm, fill_hbm,
    new_ref, grown_ref,
    movie, foot, block_ref, neuron_ref, fill_ref,
    all_traces, side_out, side_in, proj_out, proj_in, back_out, back_in,
    num_out, num_in, pow_out, pow_in,
    local_sem, send_sem, recv_sem, side_send, side_recv, tm_send, tm_recv,
):
    me = lax.axis_index("pix")
    core = lax.axis_index("tm")
    slots = foot.shape[0]
    cap = slots // n
    neur = traces_hbm.shape[0]
    frames = movie.shape[1]
    blocks = movie.shape[0] // BLOCK
    neurons = n * neur
    wide = frames // PARTS
    pieces = range(PARTS)

    def pix_id(peer):
        return (peer, core)

    def peers(body):
        if n <= 16:
            for k in near_order(n):
                body(lax.rem(me + k, n))
        else:
            lax.fori_loop(1, n, lambda k, _: (body(lax.rem(me + k, n)), 0)[1], 0)

    def part(index, size):
        return pl.ds(pl.multiple_of(index * size, size), size)

    barrier = pltpu.get_barrier_semaphore()
    peers(lambda p: pl.semaphore_signal(barrier, inc=1, device_id=pix_id(p)))
    for k in range(1, t):
        pl.semaphore_signal(barrier, inc=1, device_id=(me, lax.rem(core + k, t)))

    def mine(h):
        return all_traces.at[h, part(me, neur)]

    def strip(h):
        return slice(h * wide, (h + 1) * wide)

    loads = [
        pltpu.make_async_copy(a, b, local_sem.at[i])
        for i, (a, b) in enumerate(
            [(traces_hbm.at[:, pl.ds(h * wide, wide)], mine(h)) for h in pieces]
            + [
                (foot_hbm, foot),
                (block_hbm, block_ref),
                (neuron_hbm, neuron_ref),
                (fill_hbm, fill_ref),
                (movie_hbm, movie),
            ]
        )
    ]
    for load in loads:
        load.start()
    for h in pieces:
        loads[h].wait()
    pl.semaphore_wait(barrier, n - 1 + t - 1)

    def trace_copy(h, p, source):
        return pltpu.make_async_remote_copy(
            src_ref=mine(h),
            dst_ref=all_traces.at[h, part(source, neur)],
            send_sem=send_sem.at[0, h, p],
            recv_sem=recv_sem.at[0, h, source],
            device_id=pix_id(p),
        )

    for h in pieces:
        peers(lambda p: trace_copy(h, p, me).start())
    for load in loads[PARTS:-1]:
        load.wait()

    diag = iota((slots, slots), 0) == iota((slots, slots), 1)

    def column(row):
        return jnp.sum(jnp.where(diag, row.astype(F32), 0.0), axis=1, keepdims=True)

    block_row = block_ref[...].astype(F32)
    block_col = column(block_row)
    neuron_col = column(neuron_ref[...])
    owner_hit = lax.div(iota((slots, n), 0), cap) == iota((slots, n), 1)
    fill_col = jnp.sum(jnp.where(owner_hit, fill_ref[...].astype(F32), 0.0), axis=1, keepdims=True)
    row_of = iota((slots, 1), 0)
    usable = lax.rem(row_of, cap).astype(F32) < fill_col
    masked = jnp.where(usable, foot[...].astype(F32), 0.0)
    masked_b = masked.astype(BF16)
    same_block = block_col == block_row
    power = jnp.sum(masked * masked, axis=1, keepdims=True)
    lane = iota((slots, LANES), 1)
    place_of = lax.rem(row_of, cap)
    side = jnp.where(
        lane == place_of, neuron_col, jnp.where(lane == place_of + ROWS, power, 0.0)
    )
    to_owner = (lax.div(iota((n, slots), 1), cap) == iota((n, slots), 0)).astype(BF16)
    side = exact_dot(to_owner, side)
    for o in range(n):
        side_out[o] = side[o : o + 1, :]

    def side_copy(p, source):
        return pltpu.make_async_remote_copy(
            src_ref=side_out.at[p],
            dst_ref=side_in.at[source],
            send_sem=side_send.at[p],
            recv_sem=side_recv.at[source],
            device_id=pix_id(p),
        )

    peers(lambda p: side_copy(p, me).start())
    side_in[me] = side_out[me]

    padded = n * ROWS
    if cap == ROWS:
        widen = narrow = lambda x: x
    else:
        slot_row = lax.div(iota((padded, slots), 0), ROWS) * cap + lax.rem(
            iota((padded, slots), 0), ROWS
        )
        real = lax.rem(iota((padded, slots), 0), ROWS) < cap
        place = ((slot_row == iota((padded, slots), 1)) & real).astype(BF16)

        def widen(x):
            return dot(place, x).astype(BF16)

        def narrow(x):
            return dot(place, x, TN).astype(BF16)

    gram = jnp.where(same_block, dot(masked_b, masked_b, NT), 0.0)
    neuron_id = lax.div(row_of, cap).astype(F32) * neur + neuron_col
    pick = (neuron_id == iota((slots, neurons), 1).astype(F32)).astype(BF16)
    gram_high, gram_low = split(gram)
    couple_high, couple_low = split(dot(gram_high, pick) + dot(gram_low, pick))

    loads[-1].wait()
    base = jnp.zeros((slots, frames), F32)
    for b in range(0, blocks, 2):
        pair = jnp.concatenate(
            [jnp.where(block_col == float(b + j), masked, 0.0).astype(BF16) for j in range(2)],
            axis=1,
        )
        base += dot(pair, movie[b * BLOCK : (b + 2) * BLOCK, :])

    def proj_copy(h, p, source):
        return pltpu.make_async_remote_copy(
            src_ref=proj_out.at[h, part(p, ROWS)],
            dst_ref=proj_in.at[h, part(source, ROWS)],
            send_sem=send_sem.at[1, h, p],
            recv_sem=recv_sem.at[1, h, source],
            device_id=pix_id(p),
        )

    for h in pieces:
        peers(lambda p: trace_copy(h, p, p).wait_recv())
        gathered = all_traces[h]
        projection = base[:, strip(h)] - (dot(couple_high, gathered) + dot(couple_low, gathered))
        proj_out[h] = widen(projection.astype(BF16))
        peers(lambda p: proj_copy(h, p, me).start())
        proj_in[h, part(me, ROWS), :] = proj_out[h, part(me, ROWS), :]

    peers(lambda p: side_copy(p, p).wait_recv())
    side_rows = jnp.concatenate([side_in[i] for i in range(n)], axis=0)
    from_tile = (lax.div(iota((padded, n), 0), ROWS) == iota((padded, n), 1)).astype(BF16)
    spread = exact_dot(from_tile, side_rows)
    spread_lane = iota((padded, LANES), 1)
    spread_place = lax.rem(iota((padded, 1), 0), ROWS)
    asked = jnp.sum(jnp.where(spread_lane == spread_place, spread, 0.0), axis=1, keepdims=True)
    asked_power = jnp.sum(
        jnp.where(spread_lane == spread_place + ROWS, spread, 0.0), axis=1, keepdims=True
    )
    hit = asked == iota((padded, neur), 1).astype(F32)
    if cap != ROWS:
        hit &= lax.rem(iota((padded, neur), 0), ROWS) < cap
    owner_pick = hit.astype(F32).astype(BF16)
    pick_turned = jnp.transpose(hit.astype(F32)).astype(BF16)
    total_power = exact_dot(pick_turned, jnp.broadcast_to(asked_power, (padded, LANES)))[:, 0:1]
    floor_power = jnp.maximum(total_power, 0.5)

    def back_copy(h, p, source):
        return pltpu.make_async_remote_copy(
            src_ref=back_out.at[h, part(p, ROWS)],
            dst_ref=back_in.at[h, part(source, ROWS)],
            send_sem=send_sem.at[2, h, p],
            recv_sem=recv_sem.at[2, h, source],
            device_id=pix_id(p),
        )

    for h in pieces:
        peers(lambda p: proj_copy(h, p, p).wait_recv())
        own = all_traces[h, part(me, neur), :].astype(F32)
        sums = dot(pick_turned, proj_in[h])
        updated = jnp.maximum(0.0, own + sums / floor_power).astype(BF16)
        back_out[h] = dot(owner_pick, updated).astype(BF16)
        peers(lambda p: back_copy(h, p, me).start())
        back_in[h, part(me, ROWS), :] = back_out[h, part(me, ROWS), :]
        new_ref[:, strip(h)] = updated

    for h in pieces:
        peers(lambda p: back_copy(h, p, p).wait_recv())
    fresh = jnp.concatenate([narrow(back_in[h]) for h in pieces], axis=1)
    fresh_f = fresh.astype(F32)
    pow_out[...] = jnp.broadcast_to(
        jnp.sum(fresh_f * fresh_f, axis=1, keepdims=True), (slots, BLOCK)
    )

    def tm_copy(index, out, into, q, source):
        return pltpu.make_async_remote_copy(
            src_ref=out,
            dst_ref=into.at[source],
            send_sem=tm_send.at[index, q],
            recv_sem=tm_recv.at[index, source],
            device_id=(me, q),
        )

    partners = [lax.rem(core + k, t) for k in range(1, t)]
    for q in partners:
        tm_copy(0, pow_out, pow_in, q, core).start()
    overlap = jnp.where(same_block, dot(fresh, fresh, NT), 0.0)
    over_high, over_low = split(overlap)
    numerator = -(dot(over_high, masked_b) + dot(over_low, masked_b))
    for b in range(0, blocks, 2):
        product = dot(fresh, movie[b * BLOCK : (b + 2) * BLOCK, :], NT)
        for j in range(2):
            numerator += jnp.where(
                block_col == float(b + j), product[:, j * BLOCK : (j + 1) * BLOCK], 0.0
            )
    num_out[...] = numerator
    for q in partners:
        tm_copy(1, num_out, num_in, q, core).start()
    pow_in[core] = pow_out[...]
    num_in[core] = numerator
    for q in partners:
        tm_copy(0, pow_out, pow_in, q, q).wait_recv()
        tm_copy(1, num_out, num_in, q, q).wait_recv()
    num_all, pow_all = num_in[0], pow_in[0]
    for q in range(1, t):
        num_all += num_in[q]
        pow_all += pow_in[q]
    grown = jnp.maximum(0.0, masked + num_all / (pow_all + 1e-06))
    grown_ref[...] = jnp.where(usable, grown, 0.0)

    peers(lambda p: side_copy(p, me).wait_send())
    for h in pieces:
        peers(lambda p: trace_copy(h, p, me).wait_send())
        peers(lambda p: proj_copy(h, p, me).wait_send())
        peers(lambda p: back_copy(h, p, me).wait_send())
    for q in partners:
        tm_copy(0, pow_out, pow_in, q, core).wait_send()
        tm_copy(1, num_out, num_in, q, core).wait_send()


def local(n, t, movie, traces, footprints, slot_block, slot_neuron, bucket_fill):
    slots = footprints.shape[0]
    neur, frames = traces.shape
    padded = n * ROWS
    wide = frames // PARTS
    return pl.pallas_call(
        functools.partial(kernel, n, t),
        out_shape=(
            jax.ShapeDtypeStruct((neur, frames), BF16),
            jax.ShapeDtypeStruct((slots, BLOCK), F32),
        ),
        in_specs=[pl.BlockSpec(memory_space=pl.ANY)] * 6,
        out_specs=[pl.BlockSpec(memory_space=pltpu.VMEM)] * 2,
        scratch_shapes=[
            pltpu.VMEM(movie.shape, BF16),
            pltpu.VMEM(footprints.shape, BF16),
            pltpu.VMEM((1, slots), jnp.int32),
            pltpu.VMEM((1, slots), jnp.int32),
            pltpu.VMEM((1, n), jnp.int32),
            pltpu.VMEM((PARTS, n * neur, wide), BF16),
            pltpu.VMEM((n, 1, LANES), F32),
            pltpu.VMEM((n, 1, LANES), F32),
            pltpu.VMEM((PARTS, padded, wide), BF16),
            pltpu.VMEM((PARTS, padded, wide), BF16),
            pltpu.VMEM((PARTS, padded, wide), BF16),
            pltpu.VMEM((PARTS, padded, wide), BF16),
            pltpu.VMEM((slots, BLOCK), F32),
            pltpu.VMEM((t, slots, BLOCK), F32),
            pltpu.VMEM((slots, BLOCK), F32),
            pltpu.VMEM((t, slots, BLOCK), F32),
            pltpu.SemaphoreType.DMA((5 + PARTS,)),
            pltpu.SemaphoreType.DMA((3, PARTS, n)),
            pltpu.SemaphoreType.DMA((3, PARTS, n)),
            pltpu.SemaphoreType.DMA((n,)),
            pltpu.SemaphoreType.DMA((n,)),
            pltpu.SemaphoreType.DMA((2, t)),
            pltpu.SemaphoreType.DMA((2, t)),
        ],
        compiler_params=pltpu.CompilerParams(
            collective_id=0, has_side_effects=True, vmem_limit_bytes=64 * 1024 * 1024 - 256 * 1024
        ),
    )(
        movie,
        traces,
        footprints,
        slot_block.reshape(1, slots),
        slot_neuron.reshape(1, slots),
        bucket_fill,
    )


def solution(mesh):
    return jax.shard_map(
        functools.partial(local, mesh.shape["pix"], mesh.shape["tm"]),
        mesh=mesh,
        in_specs=(
            P("pix", "tm"),
            P("pix", "tm"),
            P("pix", None),
            P("pix"),
            P("pix"),
            P("pix", None),
        ),
        out_specs=(P("pix", "tm"), P("pix", None)),
        check_vma=False,
    )
```

```python
import functools

import jax
import jax.numpy as jnp
from jax import lax
from jax.experimental import pallas as pl
from jax.experimental.pallas import tpu as pltpu
from jax.sharding import PartitionSpec as P

BLOCK = 128
ROWS = 16
LANES = 128
PARTS = 2
F32 = jnp.float32
BF16 = jnp.bfloat16
NN = (((1,), (0,)), ((), ()))
NT = (((1,), (1,)), ((), ()))
TN = (((0,), (0,)), ((), ()))


def dot(a, b, dims=NN):
    return lax.dot_general(a, b, dims, preferred_element_type=F32)


def split(value):
    high = value.astype(BF16)
    return high, (value - high.astype(F32)).astype(BF16)


def exact_dot(ones, b):
    high, rest = b.astype(BF16), b - b.astype(BF16).astype(F32)
    mid, low = split(rest)
    return dot(ones, high) + dot(ones, mid) + dot(ones, low)


def iota(shape, dim):
    return lax.broadcasted_iota(jnp.int32, shape, dim)


def near_order(n):
    return sorted(range(1, n), key=lambda k: (abs(k - n // 2), k))


def kernel(
    n, t, movie_hbm, traces_hbm, foot_hbm, block_hbm, neuron_hbm, fill_hbm,
    new_ref, grown_ref,
    movie, foot, block_ref, neuron_ref, fill_ref,
    all_traces, side_out, side_in, proj_out, proj_in, back_out, back_in,
    num_out, num_in, pow_out, pow_in,
    local_sem, send_sem, recv_sem, side_send, side_recv, tm_send, tm_recv,
):
    me = lax.axis_index("pix")
    core = lax.axis_index("tm")
    slots = foot.shape[0]
    cap = slots // n
    neur = traces_hbm.shape[0]
    frames = movie.shape[1]
    blocks = movie.shape[0] // BLOCK
    neurons = n * neur
    wide = frames // PARTS
    pieces = range(PARTS)

    def pix_id(peer):
        return (peer, core)

    def peers(body):
        if n <= 16:
            for k in near_order(n):
                body(lax.rem(me + k, n))
        else:
            lax.fori_loop(1, n, lambda k, _: (body(lax.rem(me + k, n)), 0)[1], 0)

    def part(index, size):
        return pl.ds(pl.multiple_of(index * size, size), size)

    barrier = pltpu.get_barrier_semaphore()
    peers(lambda p: pl.semaphore_signal(barrier, inc=1, device_id=pix_id(p)))
    for k in range(1, t):
        pl.semaphore_signal(barrier, inc=1, device_id=(me, lax.rem(core + k, t)))

    def mine(h):
        return all_traces.at[h, part(me, neur)]

    def strip(h):
        return slice(h * wide, (h + 1) * wide)

    loads = [
        pltpu.make_async_copy(a, b, local_sem.at[i])
        for i, (a, b) in enumerate(
            [(traces_hbm.at[:, pl.ds(h * wide, wide)], mine(h)) for h in pieces]
            + [
                (foot_hbm, foot),
                (block_hbm, block_ref),
                (neuron_hbm, neuron_ref),
                (fill_hbm, fill_ref),
                (movie_hbm, movie),
            ]
        )
    ]
    for load in loads:
        load.start()
    for h in pieces:
        loads[h].wait()
    pl.semaphore_wait(barrier, n - 1 + t - 1)

    def trace_copy(h, p, source):
        return pltpu.make_async_remote_copy(
            src_ref=mine(h),
            dst_ref=all_traces.at[h, part(source, neur)],
            send_sem=send_sem.at[0, h, p],
            recv_sem=recv_sem.at[0, h, source],
            device_id=pix_id(p),
        )

    for h in pieces:
        peers(lambda p: trace_copy(h, p, me).start())
    for load in loads[PARTS:-1]:
        load.wait()

    diag = iota((slots, slots), 0) == iota((slots, slots), 1)

    def column(row):
        return jnp.sum(jnp.where(diag, row.astype(F32), 0.0), axis=1, keepdims=True)

    block_row = block_ref[...].astype(F32)
    block_col = column(block_row)
    neuron_col = column(neuron_ref[...])
    owner_hit = lax.div(iota((slots, n), 0), cap) == iota((slots, n), 1)
    fill_col = jnp.sum(jnp.where(owner_hit, fill_ref[...].astype(F32), 0.0), axis=1, keepdims=True)
    row_of = iota((slots, 1), 0)
    usable = lax.rem(row_of, cap).astype(F32) < fill_col
    masked = jnp.where(usable, foot[...].astype(F32), 0.0)
    masked_b = masked.astype(BF16)
    same_block = block_col == block_row
    power = jnp.sum(masked * masked, axis=1, keepdims=True)
    lane = iota((slots, LANES), 1)
    place_of = lax.rem(row_of, cap)
    side = jnp.where(
        lane == place_of, neuron_col, jnp.where(lane == place_of + ROWS, power, 0.0)
    )
    to_owner = (lax.div(iota((n, slots), 1), cap) == iota((n, slots), 0)).astype(BF16)
    side = exact_dot(to_owner, side)
    for o in range(n):
        side_out[o] = side[o : o + 1, :]

    def side_copy(p, source):
        return pltpu.make_async_remote_copy(
            src_ref=side_out.at[p],
            dst_ref=side_in.at[source],
            send_sem=side_send.at[p],
            recv_sem=side_recv.at[source],
            device_id=pix_id(p),
        )

    peers(lambda p: side_copy(p, me).start())
    side_in[me] = side_out[me]

    padded = n * ROWS
    if cap == ROWS:
        widen = narrow = lambda x: x
    else:
        slot_row = lax.div(iota((padded, slots), 0), ROWS) * cap + lax.rem(
            iota((padded, slots), 0), ROWS
        )
        real = lax.rem(iota((padded, slots), 0), ROWS) < cap
        place = ((slot_row == iota((padded, slots), 1)) & real).astype(BF16)

        def widen(x):
            return dot(place, x).astype(BF16)

        def narrow(x):
            return dot(place, x, TN).astype(BF16)

    gram = jnp.where(same_block, dot(masked_b, masked_b, NT), 0.0)
    neuron_id = lax.div(row_of, cap).astype(F32) * neur + neuron_col
    pick = (neuron_id == iota((slots, neurons), 1).astype(F32)).astype(BF16)
    gram_high, gram_low = split(gram)
    couple_high, couple_low = split(dot(gram_high, pick) + dot(gram_low, pick))

    loads[-1].wait()
    base = jnp.zeros((slots, frames), F32)
    for b in range(0, blocks, 2):
        pair = jnp.concatenate(
            [jnp.where(block_col == float(b + j), masked, 0.0).astype(BF16) for j in range(2)],
            axis=1,
        )
        base += dot(pair, movie[b * BLOCK : (b + 2) * BLOCK, :])

    def proj_copy(h, p, source):
        return pltpu.make_async_remote_copy(
            src_ref=proj_out.at[h, part(p, ROWS)],
            dst_ref=proj_in.at[h, part(source, ROWS)],
            send_sem=send_sem.at[1, h, p],
            recv_sem=recv_sem.at[1, h, source],
            device_id=pix_id(p),
        )

    for h in pieces:
        peers(lambda p: trace_copy(h, p, p).wait_recv())
        gathered = all_traces[h]
        projection = base[:, strip(h)] - (dot(couple_high, gathered) + dot(couple_low, gathered))
        proj_out[h] = widen(projection.astype(BF16))
        peers(lambda p: proj_copy(h, p, me).start())
        proj_in[h, part(me, ROWS), :] = proj_out[h, part(me, ROWS), :]

    peers(lambda p: side_copy(p, p).wait_recv())
    side_rows = jnp.concatenate([side_in[i] for i in range(n)], axis=0)
    from_tile = (lax.div(iota((padded, n), 0), ROWS) == iota((padded, n), 1)).astype(BF16)
    spread = exact_dot(from_tile, side_rows)
    spread_lane = iota((padded, LANES), 1)
    spread_place = lax.rem(iota((padded, 1), 0), ROWS)
    asked = jnp.sum(jnp.where(spread_lane == spread_place, spread, 0.0), axis=1, keepdims=True)
    asked_power = jnp.sum(
        jnp.where(spread_lane == spread_place + ROWS, spread, 0.0), axis=1, keepdims=True
    )
    hit = asked == iota((padded, neur), 1).astype(F32)
    if cap != ROWS:
        hit &= lax.rem(iota((padded, neur), 0), ROWS) < cap
    owner_pick = hit.astype(F32).astype(BF16)
    pick_turned = jnp.transpose(hit.astype(F32)).astype(BF16)
    total_power = exact_dot(pick_turned, jnp.broadcast_to(asked_power, (padded, LANES)))[:, 0:1]
    floor_power = jnp.maximum(total_power, 0.5)

    def back_copy(h, p, source):
        return pltpu.make_async_remote_copy(
            src_ref=back_out.at[h, part(p, ROWS)],
            dst_ref=back_in.at[h, part(source, ROWS)],
            send_sem=send_sem.at[2, h, p],
            recv_sem=recv_sem.at[2, h, source],
            device_id=pix_id(p),
        )

    for h in pieces:
        peers(lambda p: proj_copy(h, p, p).wait_recv())
        own = all_traces[h, part(me, neur), :].astype(F32)
        sums = dot(pick_turned, proj_in[h])
        updated = jnp.maximum(0.0, own + sums / floor_power).astype(BF16)
        back_out[h] = dot(owner_pick, updated).astype(BF16)
        peers(lambda p: back_copy(h, p, me).start())
        back_in[h, part(me, ROWS), :] = back_out[h, part(me, ROWS), :]
        new_ref[:, strip(h)] = updated

    for h in pieces:
        peers(lambda p: back_copy(h, p, p).wait_recv())
    fresh = jnp.concatenate([narrow(back_in[h]) for h in pieces], axis=1)
    fresh_f = fresh.astype(F32)
    pow_out[...] = jnp.broadcast_to(
        jnp.sum(fresh_f * fresh_f, axis=1, keepdims=True), (slots, BLOCK)
    )

    def tm_copy(index, out, into, q, source):
        return pltpu.make_async_remote_copy(
            src_ref=out,
            dst_ref=into.at[source],
            send_sem=tm_send.at[index, q],
            recv_sem=tm_recv.at[index, source],
            device_id=(me, q),
        )

    partners = [lax.rem(core + k, t) for k in range(1, t)]
    for q in partners:
        tm_copy(0, pow_out, pow_in, q, core).start()
    overlap = jnp.where(same_block, dot(fresh, fresh, NT), 0.0)
    over_high, over_low = split(overlap)
    numerator = -(dot(over_high, masked_b) + dot(over_low, masked_b))
    for b in range(0, blocks, 2):
        product = dot(fresh, movie[b * BLOCK : (b + 2) * BLOCK, :], NT)
        for j in range(2):
            numerator += jnp.where(
                block_col == float(b + j), product[:, j * BLOCK : (j + 1) * BLOCK], 0.0
            )
    num_out[...] = numerator
    for q in partners:
        tm_copy(1, num_out, num_in, q, core).start()
    pow_in[core] = pow_out[...]
    num_in[core] = numerator
    for q in partners:
        tm_copy(0, pow_out, pow_in, q, q).wait_recv()
        tm_copy(1, num_out, num_in, q, q).wait_recv()
    num_all, pow_all = num_in[0], pow_in[0]
    for q in range(1, t):
        num_all += num_in[q]
        pow_all += pow_in[q]
    grown = jnp.maximum(0.0, masked + num_all / (pow_all + 1e-06))
    grown_ref[...] = jnp.where(usable, grown, 0.0)

    peers(lambda p: side_copy(p, me).wait_send())
    for h in pieces:
        peers(lambda p: trace_copy(h, p, me).wait_send())
        peers(lambda p: proj_copy(h, p, me).wait_send())
        peers(lambda p: back_copy(h, p, me).wait_send())
    for q in partners:
        tm_copy(0, pow_out, pow_in, q, core).wait_send()
        tm_copy(1, num_out, num_in, q, core).wait_send()


def local(n, t, movie, traces, footprints, slot_block, slot_neuron, bucket_fill):
    slots = footprints.shape[0]
    neur, frames = traces.shape
    padded = n * ROWS
    wide = frames // PARTS
    return pl.pallas_call(
        functools.partial(kernel, n, t),
        out_shape=(
            jax.ShapeDtypeStruct((neur, frames), BF16),
            jax.ShapeDtypeStruct((slots, BLOCK), F32),
        ),
        in_specs=[pl.BlockSpec(memory_space=pl.ANY)] * 6,
        out_specs=[pl.BlockSpec(memory_space=pltpu.VMEM)] * 2,
        scratch_shapes=[
            pltpu.VMEM(movie.shape, BF16),
            pltpu.VMEM(footprints.shape, BF16),
            pltpu.VMEM((1, slots), jnp.int32),
            pltpu.VMEM((1, slots), jnp.int32),
            pltpu.VMEM((1, n), jnp.int32),
            pltpu.VMEM((PARTS, n * neur, wide), BF16),
            pltpu.VMEM((n, 1, LANES), F32),
            pltpu.VMEM((n, 1, LANES), F32),
            pltpu.VMEM((PARTS, padded, wide), BF16),
            pltpu.VMEM((PARTS, padded, wide), BF16),
            pltpu.VMEM((PARTS, padded, wide), BF16),
            pltpu.VMEM((PARTS, padded, wide), BF16),
            pltpu.VMEM((slots, BLOCK), F32),
            pltpu.VMEM((t, slots, BLOCK), F32),
            pltpu.VMEM((slots, BLOCK), F32),
            pltpu.VMEM((t, slots, BLOCK), F32),
            pltpu.SemaphoreType.DMA((5 + PARTS,)),
            pltpu.SemaphoreType.DMA((3, PARTS, n)),
            pltpu.SemaphoreType.DMA((3, PARTS, n)),
            pltpu.SemaphoreType.DMA((n,)),
            pltpu.SemaphoreType.DMA((n,)),
            pltpu.SemaphoreType.DMA((2, t)),
            pltpu.SemaphoreType.DMA((2, t)),
        ],
        compiler_params=pltpu.CompilerParams(
            collective_id=0, has_side_effects=True, vmem_limit_bytes=64 * 1024 * 1024 - 256 * 1024
        ),
    )(
        movie,
        traces,
        footprints,
        slot_block.reshape(1, slots),
        slot_neuron.reshape(1, slots),
        bucket_fill,
    )


def solution(mesh):
    return jax.shard_map(
        functools.partial(local, mesh.shape["pix"], mesh.shape["tm"]),
        mesh=mesh,
        in_specs=(
            P("pix", "tm"),
            P("pix", "tm"),
            P("pix", None),
            P("pix"),
            P("pix"),
            P("pix", None),
        ),
        out_specs=(P("pix", "tm"), P("pix", None)),
        check_vma=False,
    )
```

```python
import functools

import jax
import jax.numpy as jnp
from jax import lax
from jax.experimental import pallas as pl
from jax.experimental.pallas import tpu as pltpu
from jax.sharding import PartitionSpec as P

BLOCK = 128
ROWS = 16
LANES = 128
PARTS = 1
VMEM_BYTES = 64 * 1024 * 1024 - 256 * 1024
F32 = jnp.float32
BF16 = jnp.bfloat16
NN = (((1,), (0,)), ((), ()))
NT = (((1,), (1,)), ((), ()))
TN = (((0,), (0,)), ((), ()))


def dot(a, b, dims=NN):
    return lax.dot_general(a, b, dims, preferred_element_type=F32)


def split(value):
    high = value.astype(BF16)
    return high, (value - high.astype(F32)).astype(BF16)


def exact_dot(ones, b):
    high, rest = b.astype(BF16), b - b.astype(BF16).astype(F32)
    mid, low = split(rest)
    return dot(ones, high) + dot(ones, mid) + dot(ones, low)


def iota(shape, dim):
    return lax.broadcasted_iota(jnp.int32, shape, dim)


def near_order(n):
    return sorted(range(1, n), key=lambda k: (abs(k - n // 2), k))


def kernel(
    n, t, movie_hbm, traces_hbm, foot_hbm, block_hbm, neuron_hbm, fill_hbm,
    new_ref, grown_ref,
    movie, foot, block_ref, neuron_ref, fill_ref,
    all_traces, side_out, side_in, proj_out, proj_in, back_out, back_in,
    num_out, num_in, pow_out, pow_in,
    local_sem, send_sem, recv_sem, side_send, side_recv, tm_send, tm_recv,
):
    me = lax.axis_index("pix")
    core = lax.axis_index("tm")
    slots = foot.shape[0]
    cap = slots // n
    neur = traces_hbm.shape[0]
    frames = movie.shape[1]
    blocks = movie.shape[0] // BLOCK
    neurons = n * neur
    wide = frames // PARTS
    pieces = range(PARTS)

    def wait_rest(ref, sem, rows):
        rest = ref.at[pl.ds(0, (n - 1) * rows)]
        pltpu.make_async_copy(rest, rest, sem).wait()

    def pix_id(peer):
        return (peer, core)

    def peers(body):
        if n <= 16:
            for k in near_order(n):
                body(lax.rem(me + k, n))
        else:
            lax.fori_loop(1, n, lambda k, _: (body(lax.rem(me + k, n)), 0)[1], 0)

    def part(index, size):
        return pl.ds(pl.multiple_of(index * size, size), size)

    barrier = pltpu.get_barrier_semaphore()
    peers(lambda p: pl.semaphore_signal(barrier, inc=1, device_id=pix_id(p)))
    for k in range(1, t):
        pl.semaphore_signal(barrier, inc=1, device_id=(me, lax.rem(core + k, t)))

    def mine(h):
        return all_traces.at[h, part(me, neur)]

    def strip(h):
        return slice(h * wide, (h + 1) * wide)

    loads = [
        pltpu.make_async_copy(a, b, local_sem.at[i])
        for i, (a, b) in enumerate(
            [(traces_hbm.at[:, pl.ds(h * wide, wide)], mine(h)) for h in pieces]
            + [
                (foot_hbm, foot),
                (block_hbm, block_ref),
                (neuron_hbm, neuron_ref),
                (fill_hbm, fill_ref),
                (movie_hbm, movie),
            ]
        )
    ]
    for load in loads:
        load.start()
    for h in pieces:
        loads[h].wait()
    pl.semaphore_wait(barrier, n - 1 + t - 1)

    def trace_copy(h, p, source):
        return pltpu.make_async_remote_copy(
            src_ref=mine(h),
            dst_ref=all_traces.at[h, part(source, neur)],
            send_sem=send_sem.at[0, h],
            recv_sem=recv_sem.at[0, h],
            device_id=pix_id(p),
        )

    for h in pieces:
        peers(lambda p: trace_copy(h, p, me).start())
    for load in loads[PARTS:-1]:
        load.wait()

    diag = iota((slots, slots), 0) == iota((slots, slots), 1)

    def column(row):
        return jnp.sum(jnp.where(diag, row.astype(F32), 0.0), axis=1, keepdims=True)

    block_row = block_ref[...].astype(F32)
    block_col = column(block_row)
    neuron_col = column(neuron_ref[...])
    owner_hit = lax.div(iota((slots, n), 0), cap) == iota((slots, n), 1)
    fill_col = jnp.sum(jnp.where(owner_hit, fill_ref[...].astype(F32), 0.0), axis=1, keepdims=True)
    row_of = iota((slots, 1), 0)
    usable = lax.rem(row_of, cap).astype(F32) < fill_col
    masked = jnp.where(usable, foot[...].astype(F32), 0.0)
    masked_b = masked.astype(BF16)
    same_block = block_col == block_row
    power = jnp.sum(masked * masked, axis=1, keepdims=True)
    lane = iota((slots, LANES), 1)
    place_of = lax.rem(row_of, cap)
    side = jnp.where(
        lane == place_of, neuron_col, jnp.where(lane == place_of + ROWS, power, 0.0)
    )
    to_owner = (lax.div(iota((n, slots), 1), cap) == iota((n, slots), 0)).astype(BF16)
    side = exact_dot(to_owner, side)
    for o in range(n):
        side_out[o] = side[o : o + 1, :]

    def side_copy(p, source):
        return pltpu.make_async_remote_copy(
            src_ref=side_out.at[p],
            dst_ref=side_in.at[source],
            send_sem=side_send.at[0],
            recv_sem=side_recv.at[0],
            device_id=pix_id(p),
        )

    peers(lambda p: side_copy(p, me).start())
    side_in[me] = side_out[me]

    padded = n * ROWS
    if cap == ROWS:
        widen = narrow = lambda x: x
    else:
        slot_row = lax.div(iota((padded, slots), 0), ROWS) * cap + lax.rem(
            iota((padded, slots), 0), ROWS
        )
        real = lax.rem(iota((padded, slots), 0), ROWS) < cap
        place = ((slot_row == iota((padded, slots), 1)) & real).astype(BF16)

        def widen(x):
            return dot(place, x).astype(BF16)

        def narrow(x):
            return dot(place, x, TN).astype(BF16)

    gram = jnp.where(same_block, dot(masked_b, masked_b, NT), 0.0)
    neuron_id = lax.div(row_of, cap).astype(F32) * neur + neuron_col
    pick = (neuron_id == iota((slots, neurons), 1).astype(F32)).astype(BF16)
    gram_high, gram_low = split(gram)
    couple_high, couple_low = split(dot(gram_high, pick) + dot(gram_low, pick))

    loads[-1].wait()
    base = jnp.zeros((slots, frames), F32)
    for b in range(0, blocks, 2):
        pair = jnp.concatenate(
            [jnp.where(block_col == float(b + j), masked, 0.0).astype(BF16) for j in range(2)],
            axis=1,
        )
        base += dot(pair, movie[b * BLOCK : (b + 2) * BLOCK, :])

    def proj_copy(h, p, source):
        return pltpu.make_async_remote_copy(
            src_ref=proj_out.at[h, part(p, ROWS)],
            dst_ref=proj_in.at[h, part(source, ROWS)],
            send_sem=send_sem.at[1, h],
            recv_sem=recv_sem.at[1, h],
            device_id=pix_id(p),
        )

    for h in pieces:
        wait_rest(all_traces.at[h], recv_sem.at[0, h], neur)
        gathered = all_traces[h]
        projection = base[:, strip(h)] - (dot(couple_high, gathered) + dot(couple_low, gathered))
        proj_out[h] = widen(projection.astype(BF16))
        peers(lambda p: proj_copy(h, p, me).start())
        proj_in[h, part(me, ROWS), :] = proj_out[h, part(me, ROWS), :]

    wait_rest(side_in, side_recv.at[0], 1)
    side_rows = jnp.concatenate([side_in[i] for i in range(n)], axis=0)
    from_tile = (lax.div(iota((padded, n), 0), ROWS) == iota((padded, n), 1)).astype(BF16)
    spread = exact_dot(from_tile, side_rows)
    spread_lane = iota((padded, LANES), 1)
    spread_place = lax.rem(iota((padded, 1), 0), ROWS)
    asked = jnp.sum(jnp.where(spread_lane == spread_place, spread, 0.0), axis=1, keepdims=True)
    asked_power = jnp.sum(
        jnp.where(spread_lane == spread_place + ROWS, spread, 0.0), axis=1, keepdims=True
    )
    hit = asked == iota((padded, neur), 1).astype(F32)
    if cap != ROWS:
        hit &= lax.rem(iota((padded, neur), 0), ROWS) < cap
    owner_pick = hit.astype(F32).astype(BF16)
    pick_turned = jnp.transpose(hit.astype(F32)).astype(BF16)
    total_power = exact_dot(pick_turned, jnp.broadcast_to(asked_power, (padded, LANES)))[:, 0:1]
    floor_power = jnp.maximum(total_power, 0.5)

    def back_copy(h, p, source):
        return pltpu.make_async_remote_copy(
            src_ref=back_out.at[h, part(p, ROWS)],
            dst_ref=back_in.at[h, part(source, ROWS)],
            send_sem=send_sem.at[2, h],
            recv_sem=recv_sem.at[2, h],
            device_id=pix_id(p),
        )

    for h in pieces:
        wait_rest(proj_in.at[h], recv_sem.at[1, h], ROWS)
        own = all_traces[h, part(me, neur), :].astype(F32)
        sums = dot(pick_turned, proj_in[h])
        updated = jnp.maximum(0.0, own + sums / floor_power).astype(BF16)
        back_out[h] = dot(owner_pick, updated).astype(BF16)
        peers(lambda p: back_copy(h, p, me).start())
        back_in[h, part(me, ROWS), :] = back_out[h, part(me, ROWS), :]
        new_ref[:, strip(h)] = updated

    for h in pieces:
        wait_rest(back_in.at[h], recv_sem.at[2, h], ROWS)
    fresh = jnp.concatenate([narrow(back_in[h]) for h in pieces], axis=1)
    fresh_f = fresh.astype(F32)
    pow_out[...] = jnp.broadcast_to(
        jnp.sum(fresh_f * fresh_f, axis=1, keepdims=True), (slots, BLOCK)
    )

    def tm_copy(index, out, into, q, source):
        return pltpu.make_async_remote_copy(
            src_ref=out,
            dst_ref=into.at[source],
            send_sem=tm_send.at[index, q],
            recv_sem=tm_recv.at[index, source],
            device_id=(me, q),
        )

    partners = [lax.rem(core + k, t) for k in range(1, t)]
    for q in partners:
        tm_copy(0, pow_out, pow_in, q, core).start()
    overlap = jnp.where(same_block, dot(fresh, fresh, NT), 0.0)
    over_high, over_low = split(overlap)
    numerator = -(dot(over_high, masked_b) + dot(over_low, masked_b))
    for b in range(0, blocks, 2):
        product = dot(fresh, movie[b * BLOCK : (b + 2) * BLOCK, :], NT)
        for j in range(2):
            numerator += jnp.where(
                block_col == float(b + j), product[:, j * BLOCK : (j + 1) * BLOCK], 0.0
            )
    num_out[...] = numerator
    for q in partners:
        tm_copy(1, num_out, num_in, q, core).start()
    pow_in[core] = pow_out[...]
    num_in[core] = numerator
    for q in partners:
        tm_copy(0, pow_out, pow_in, q, q).wait_recv()
        tm_copy(1, num_out, num_in, q, q).wait_recv()
    num_all, pow_all = num_in[0], pow_in[0]
    for q in range(1, t):
        num_all += num_in[q]
        pow_all += pow_in[q]
    grown = jnp.maximum(0.0, masked + num_all / (pow_all + 1e-06))
    grown_ref[...] = jnp.where(usable, grown, 0.0)

    wait_rest(side_out, side_send.at[0], 1)
    for h in pieces:
        wait_rest(all_traces.at[h], send_sem.at[0, h], neur)
        wait_rest(proj_out.at[h], send_sem.at[1, h], ROWS)
        wait_rest(back_out.at[h], send_sem.at[2, h], ROWS)
    for q in partners:
        tm_copy(0, pow_out, pow_in, q, core).wait_send()
        tm_copy(1, num_out, num_in, q, core).wait_send()


def settle(new_in, grown_in, new_out, grown_out, sem):
    moves = [
        pltpu.make_async_copy(new_in, new_out, sem.at[0]),
        pltpu.make_async_copy(grown_in, grown_out, sem.at[1]),
    ]
    for move in moves:
        move.start()
    for move in moves:
        move.wait()


def local(n, t, movie, traces, footprints, slot_block, slot_neuron, bucket_fill):
    slots = footprints.shape[0]
    neur, frames = traces.shape
    padded = n * ROWS
    wide = frames // PARTS
    results = (
        jax.ShapeDtypeStruct((neur, frames), BF16),
        jax.ShapeDtypeStruct((slots, BLOCK), F32),
    )
    swept = pl.pallas_call(
        functools.partial(kernel, n, t),
        out_shape=results,
        in_specs=[pl.BlockSpec(memory_space=pl.ANY)] * 6,
        out_specs=[pl.BlockSpec(memory_space=pltpu.VMEM)] * 2,
        scratch_shapes=[
            pltpu.VMEM(movie.shape, BF16),
            pltpu.VMEM(footprints.shape, BF16),
            pltpu.VMEM((1, slots), jnp.int32),
            pltpu.VMEM((1, slots), jnp.int32),
            pltpu.VMEM((1, n), jnp.int32),
            pltpu.VMEM((PARTS, n * neur, wide), BF16),
            pltpu.VMEM((n, 1, LANES), F32),
            pltpu.VMEM((n, 1, LANES), F32),
            pltpu.VMEM((PARTS, padded, wide), BF16),
            pltpu.VMEM((PARTS, padded, wide), BF16),
            pltpu.VMEM((PARTS, padded, wide), BF16),
            pltpu.VMEM((PARTS, padded, wide), BF16),
            pltpu.VMEM((slots, BLOCK), F32),
            pltpu.VMEM((t, slots, BLOCK), F32),
            pltpu.VMEM((slots, BLOCK), F32),
            pltpu.VMEM((t, slots, BLOCK), F32),
            pltpu.SemaphoreType.DMA((5 + PARTS,)),
            pltpu.SemaphoreType.DMA((3, PARTS)),
            pltpu.SemaphoreType.DMA((3, PARTS)),
            pltpu.SemaphoreType.DMA((1,)),
            pltpu.SemaphoreType.DMA((1,)),
            pltpu.SemaphoreType.DMA((2, t)),
            pltpu.SemaphoreType.DMA((2, t)),
        ],
        compiler_params=pltpu.CompilerParams(
            collective_id=0, has_side_effects=True, vmem_limit_bytes=VMEM_BYTES
        ),
    )(
        movie,
        traces,
        footprints,
        slot_block.reshape(1, slots),
        slot_neuron.reshape(1, slots),
        bucket_fill,
    )
    return pl.pallas_call(
        settle,
        out_shape=results,
        in_specs=[pl.BlockSpec(memory_space=pl.ANY)] * 2,
        out_specs=[pl.BlockSpec(memory_space=pl.ANY)] * 2,
        scratch_shapes=[pltpu.SemaphoreType.DMA((2,))],
        compiler_params=pltpu.CompilerParams(vmem_limit_bytes=VMEM_BYTES),
    )(*swept)


def solution(mesh):
    return jax.shard_map(
        functools.partial(local, mesh.shape["pix"], mesh.shape["tm"]),
        mesh=mesh,
        in_specs=(
            P("pix", "tm"),
            P("pix", "tm"),
            P("pix", None),
            P("pix"),
            P("pix"),
            P("pix", None),
        ),
        out_specs=(P("pix", "tm"), P("pix", None)),
        check_vma=False,
    )
```

```python
import functools

import jax
import jax.numpy as jnp
from jax import lax
from jax.experimental import pallas as pl
from jax.experimental.pallas import tpu as pltpu
from jax.sharding import PartitionSpec as P

BLOCK = 128
ROWS = 16
LANES = 128
PARTS = 2
VMEM_BYTES = 64 * 1024 * 1024 - 256 * 1024
F32 = jnp.float32
BF16 = jnp.bfloat16
NN = (((1,), (0,)), ((), ()))
NT = (((1,), (1,)), ((), ()))
TN = (((0,), (0,)), ((), ()))


def dot(a, b, dims=NN):
    return lax.dot_general(a, b, dims, preferred_element_type=F32)


def split(value):
    high = value.astype(BF16)
    return high, (value - high.astype(F32)).astype(BF16)


def exact_dot(ones, b):
    high, rest = b.astype(BF16), b - b.astype(BF16).astype(F32)
    mid, low = split(rest)
    return dot(ones, high) + dot(ones, mid) + dot(ones, low)


def iota(shape, dim):
    return lax.broadcasted_iota(jnp.int32, shape, dim)


def near_order(n):
    return sorted(range(1, n), key=lambda k: (abs(k - n // 2), k))


def kernel(
    n, t, movie_hbm, traces_hbm, foot_hbm, block_hbm, neuron_hbm, fill_hbm,
    new_ref, grown_ref,
    movie, foot, block_ref, neuron_ref, fill_ref,
    all_traces, side_out, side_in, proj_out, proj_in, back_out, back_in,
    num_out, num_in, pow_out, pow_in,
    local_sem, send_sem, recv_sem, side_send, side_recv, tm_send, tm_recv,
):
    me = lax.axis_index("pix")
    core = lax.axis_index("tm")
    slots = foot.shape[0]
    cap = slots // n
    neur = traces_hbm.shape[0]
    frames = movie.shape[1]
    blocks = movie.shape[0] // BLOCK
    neurons = n * neur
    wide = frames // PARTS
    pieces = range(PARTS)

    def wait_rest(ref, sem, rows):
        rest = ref.at[pl.ds(0, (n - 1) * rows)]
        pltpu.make_async_copy(rest, rest, sem).wait()

    def pix_id(peer):
        return (peer, core)

    def peers(body):
        if n <= 16:
            for k in near_order(n):
                body(lax.rem(me + k, n))
        else:
            lax.fori_loop(1, n, lambda k, _: (body(lax.rem(me + k, n)), 0)[1], 0)

    def part(index, size):
        return pl.ds(pl.multiple_of(index * size, size), size)

    barrier = pltpu.get_barrier_semaphore()
    peers(lambda p: pl.semaphore_signal(barrier, inc=1, device_id=pix_id(p)))
    for k in range(1, t):
        pl.semaphore_signal(barrier, inc=1, device_id=(me, lax.rem(core + k, t)))

    def mine(h):
        return all_traces.at[h, part(me, neur)]

    def strip(h):
        return slice(h * wide, (h + 1) * wide)

    loads = [
        pltpu.make_async_copy(a, b, local_sem.at[i])
        for i, (a, b) in enumerate(
            [(traces_hbm.at[:, pl.ds(h * wide, wide)], mine(h)) for h in pieces]
            + [
                (foot_hbm, foot),
                (block_hbm, block_ref),
                (neuron_hbm, neuron_ref),
                (fill_hbm, fill_ref),
                (movie_hbm, movie),
            ]
        )
    ]
    for load in loads:
        load.start()
    for h in pieces:
        loads[h].wait()
    pl.semaphore_wait(barrier, n - 1 + t - 1)

    def trace_copy(h, p, source):
        return pltpu.make_async_remote_copy(
            src_ref=mine(h),
            dst_ref=all_traces.at[h, part(source, neur)],
            send_sem=send_sem.at[0, h],
            recv_sem=recv_sem.at[0, h],
            device_id=pix_id(p),
        )

    for h in pieces:
        peers(lambda p: trace_copy(h, p, me).start())
    for load in loads[PARTS:-1]:
        load.wait()

    diag = iota((slots, slots), 0) == iota((slots, slots), 1)

    def column(row):
        return jnp.sum(jnp.where(diag, row.astype(F32), 0.0), axis=1, keepdims=True)

    block_row = block_ref[...].astype(F32)
    block_col = column(block_row)
    neuron_col = column(neuron_ref[...])
    owner_hit = lax.div(iota((slots, n), 0), cap) == iota((slots, n), 1)
    fill_col = jnp.sum(jnp.where(owner_hit, fill_ref[...].astype(F32), 0.0), axis=1, keepdims=True)
    row_of = iota((slots, 1), 0)
    usable = lax.rem(row_of, cap).astype(F32) < fill_col
    masked = jnp.where(usable, foot[...].astype(F32), 0.0)
    masked_b = masked.astype(BF16)
    same_block = block_col == block_row
    power = jnp.sum(masked * masked, axis=1, keepdims=True)
    lane = iota((slots, LANES), 1)
    place_of = lax.rem(row_of, cap)
    side = jnp.where(
        lane == place_of, neuron_col, jnp.where(lane == place_of + ROWS, power, 0.0)
    )
    to_owner = (lax.div(iota((n, slots), 1), cap) == iota((n, slots), 0)).astype(BF16)
    side = exact_dot(to_owner, side)
    for o in range(n):
        side_out[o] = side[o : o + 1, :]

    def side_copy(p, source):
        return pltpu.make_async_remote_copy(
            src_ref=side_out.at[p],
            dst_ref=side_in.at[source],
            send_sem=side_send.at[0],
            recv_sem=side_recv.at[0],
            device_id=pix_id(p),
        )

    peers(lambda p: side_copy(p, me).start())
    side_in[me] = side_out[me]

    padded = n * ROWS
    if cap == ROWS:
        widen = narrow = lambda x: x
    else:
        slot_row = lax.div(iota((padded, slots), 0), ROWS) * cap + lax.rem(
            iota((padded, slots), 0), ROWS
        )
        real = lax.rem(iota((padded, slots), 0), ROWS) < cap
        place = ((slot_row == iota((padded, slots), 1)) & real).astype(BF16)

        def widen(x):
            return dot(place, x).astype(BF16)

        def narrow(x):
            return dot(place, x, TN).astype(BF16)

    gram = jnp.where(same_block, dot(masked_b, masked_b, NT), 0.0)
    neuron_id = lax.div(row_of, cap).astype(F32) * neur + neuron_col
    pick = (neuron_id == iota((slots, neurons), 1).astype(F32)).astype(BF16)
    gram_high, gram_low = split(gram)
    couple_high, couple_low = split(dot(gram_high, pick) + dot(gram_low, pick))

    loads[-1].wait()
    base = jnp.zeros((slots, frames), F32)
    for b in range(0, blocks, 2):
        pair = jnp.concatenate(
            [jnp.where(block_col == float(b + j), masked, 0.0).astype(BF16) for j in range(2)],
            axis=1,
        )
        base += dot(pair, movie[b * BLOCK : (b + 2) * BLOCK, :])

    def proj_copy(h, p, source):
        return pltpu.make_async_remote_copy(
            src_ref=proj_out.at[h, part(p, ROWS)],
            dst_ref=proj_in.at[h, part(source, ROWS)],
            send_sem=send_sem.at[1, h],
            recv_sem=recv_sem.at[1, h],
            device_id=pix_id(p),
        )

    for h in pieces:
        wait_rest(all_traces.at[h], recv_sem.at[0, h], neur)
        gathered = all_traces[h]
        projection = base[:, strip(h)] - (dot(couple_high, gathered) + dot(couple_low, gathered))
        proj_out[h] = widen(projection.astype(BF16))
        peers(lambda p: proj_copy(h, p, me).start())
        proj_in[h, part(me, ROWS), :] = proj_out[h, part(me, ROWS), :]

    wait_rest(side_in, side_recv.at[0], 1)
    side_rows = jnp.concatenate([side_in[i] for i in range(n)], axis=0)
    from_tile = (lax.div(iota((padded, n), 0), ROWS) == iota((padded, n), 1)).astype(BF16)
    spread = exact_dot(from_tile, side_rows)
    spread_lane = iota((padded, LANES), 1)
    spread_place = lax.rem(iota((padded, 1), 0), ROWS)
    asked = jnp.sum(jnp.where(spread_lane == spread_place, spread, 0.0), axis=1, keepdims=True)
    asked_power = jnp.sum(
        jnp.where(spread_lane == spread_place + ROWS, spread, 0.0), axis=1, keepdims=True
    )
    hit = asked == iota((padded, neur), 1).astype(F32)
    if cap != ROWS:
        hit &= lax.rem(iota((padded, neur), 0), ROWS) < cap
    owner_pick = hit.astype(F32).astype(BF16)
    pick_turned = jnp.transpose(hit.astype(F32)).astype(BF16)
    total_power = exact_dot(pick_turned, jnp.broadcast_to(asked_power, (padded, LANES)))[:, 0:1]
    floor_power = jnp.maximum(total_power, 0.5)

    def back_copy(h, p, source):
        return pltpu.make_async_remote_copy(
            src_ref=back_out.at[h, part(p, ROWS)],
            dst_ref=back_in.at[h, part(source, ROWS)],
            send_sem=send_sem.at[2, h],
            recv_sem=recv_sem.at[2, h],
            device_id=pix_id(p),
        )

    for h in pieces:
        wait_rest(proj_in.at[h], recv_sem.at[1, h], ROWS)
        own = all_traces[h, part(me, neur), :].astype(F32)
        sums = dot(pick_turned, proj_in[h])
        updated = jnp.maximum(0.0, own + sums / floor_power).astype(BF16)
        back_out[h] = dot(owner_pick, updated).astype(BF16)
        peers(lambda p: back_copy(h, p, me).start())
        back_in[h, part(me, ROWS), :] = back_out[h, part(me, ROWS), :]
        new_ref[:, strip(h)] = updated

    for h in pieces:
        wait_rest(back_in.at[h], recv_sem.at[2, h], ROWS)
    fresh = jnp.concatenate([narrow(back_in[h]) for h in pieces], axis=1)
    fresh_f = fresh.astype(F32)
    pow_out[...] = jnp.broadcast_to(
        jnp.sum(fresh_f * fresh_f, axis=1, keepdims=True), (slots, BLOCK)
    )

    def tm_copy(index, out, into, q, source):
        return pltpu.make_async_remote_copy(
            src_ref=out,
            dst_ref=into.at[source],
            send_sem=tm_send.at[index, q],
            recv_sem=tm_recv.at[index, source],
            device_id=(me, q),
        )

    partners = [lax.rem(core + k, t) for k in range(1, t)]
    for q in partners:
        tm_copy(0, pow_out, pow_in, q, core).start()
    overlap = jnp.where(same_block, dot(fresh, fresh, NT), 0.0)
    over_high, over_low = split(overlap)
    numerator = -(dot(over_high, masked_b) + dot(over_low, masked_b))
    for b in range(0, blocks, 2):
        product = dot(fresh, movie[b * BLOCK : (b + 2) * BLOCK, :], NT)
        for j in range(2):
            numerator += jnp.where(
                block_col == float(b + j), product[:, j * BLOCK : (j + 1) * BLOCK], 0.0
            )
    num_out[...] = numerator
    for q in partners:
        tm_copy(1, num_out, num_in, q, core).start()
    pow_in[core] = pow_out[...]
    num_in[core] = numerator
    for q in partners:
        tm_copy(0, pow_out, pow_in, q, q).wait_recv()
        tm_copy(1, num_out, num_in, q, q).wait_recv()
    num_all, pow_all = num_in[0], pow_in[0]
    for q in range(1, t):
        num_all += num_in[q]
        pow_all += pow_in[q]
    grown = jnp.maximum(0.0, masked + num_all / (pow_all + 1e-06))
    grown_ref[...] = jnp.where(usable, grown, 0.0)

    wait_rest(side_out, side_send.at[0], 1)
    for h in pieces:
        wait_rest(all_traces.at[h], send_sem.at[0, h], neur)
        wait_rest(proj_out.at[h], send_sem.at[1, h], ROWS)
        wait_rest(back_out.at[h], send_sem.at[2, h], ROWS)
    for q in partners:
        tm_copy(0, pow_out, pow_in, q, core).wait_send()
        tm_copy(1, num_out, num_in, q, core).wait_send()


def settle(new_in, grown_in, new_out, grown_out):
    new_out[...] = new_in[...]
    grown_out[...] = grown_in[...]


def local(n, t, movie, traces, footprints, slot_block, slot_neuron, bucket_fill):
    slots = footprints.shape[0]
    neur, frames = traces.shape
    padded = n * ROWS
    wide = frames // PARTS
    results = (
        jax.ShapeDtypeStruct((neur, frames), BF16),
        jax.ShapeDtypeStruct((slots, BLOCK), F32),
    )
    swept = pl.pallas_call(
        functools.partial(kernel, n, t),
        out_shape=results,
        in_specs=[pl.BlockSpec(memory_space=pl.ANY)] * 6,
        out_specs=[pl.BlockSpec(memory_space=pltpu.VMEM)] * 2,
        scratch_shapes=[
            pltpu.VMEM(movie.shape, BF16),
            pltpu.VMEM(footprints.shape, BF16),
            pltpu.VMEM((1, slots), jnp.int32),
            pltpu.VMEM((1, slots), jnp.int32),
            pltpu.VMEM((1, n), jnp.int32),
            pltpu.VMEM((PARTS, n * neur, wide), BF16),
            pltpu.VMEM((n, 1, LANES), F32),
            pltpu.VMEM((n, 1, LANES), F32),
            pltpu.VMEM((PARTS, padded, wide), BF16),
            pltpu.VMEM((PARTS, padded, wide), BF16),
            pltpu.VMEM((PARTS, padded, wide), BF16),
            pltpu.VMEM((PARTS, padded, wide), BF16),
            pltpu.VMEM((slots, BLOCK), F32),
            pltpu.VMEM((t, slots, BLOCK), F32),
            pltpu.VMEM((slots, BLOCK), F32),
            pltpu.VMEM((t, slots, BLOCK), F32),
            pltpu.SemaphoreType.DMA((5 + PARTS,)),
            pltpu.SemaphoreType.DMA((3, PARTS)),
            pltpu.SemaphoreType.DMA((3, PARTS)),
            pltpu.SemaphoreType.DMA((1,)),
            pltpu.SemaphoreType.DMA((1,)),
            pltpu.SemaphoreType.DMA((2, t)),
            pltpu.SemaphoreType.DMA((2, t)),
        ],
        compiler_params=pltpu.CompilerParams(
            collective_id=0, has_side_effects=True, vmem_limit_bytes=VMEM_BYTES
        ),
    )(
        movie,
        traces,
        footprints,
        slot_block.reshape(1, slots),
        slot_neuron.reshape(1, slots),
        bucket_fill,
    )
    return pl.pallas_call(
        settle,
        out_shape=results,
        in_specs=[pl.BlockSpec(memory_space=pltpu.VMEM)] * 2,
        out_specs=[pl.BlockSpec(memory_space=pltpu.VMEM)] * 2,
        compiler_params=pltpu.CompilerParams(vmem_limit_bytes=VMEM_BYTES),
    )(*swept)


def solution(mesh):
    return jax.shard_map(
        functools.partial(local, mesh.shape["pix"], mesh.shape["tm"]),
        mesh=mesh,
        in_specs=(
            P("pix", "tm"),
            P("pix", "tm"),
            P("pix", None),
            P("pix"),
            P("pix"),
            P("pix", None),
        ),
        out_specs=(P("pix", "tm"), P("pix", None)),
        check_vma=False,
    )
```

```python
import functools

import jax
import jax.numpy as jnp
from jax import lax
from jax.experimental import pallas as pl
from jax.experimental.pallas import tpu as pltpu
from jax.sharding import PartitionSpec as P

BLOCK = 128
ROWS = 16
LANES = 128
PARTS = 2
PLANE = 4
VMEM_BYTES = 64 * 1024 * 1024 - 256 * 1024
F32 = jnp.float32
BF16 = jnp.bfloat16
NN = (((1,), (0,)), ((), ()))
NT = (((1,), (1,)), ((), ()))
TN = (((0,), (0,)), ((), ()))


def dot(a, b, dims=NN):
    return lax.dot_general(a, b, dims, preferred_element_type=F32)


def split(value):
    high = value.astype(BF16)
    return high, (value - high.astype(F32)).astype(BF16)


def exact_dot(ones, b):
    high, rest = b.astype(BF16), b - b.astype(BF16).astype(F32)
    mid, low = split(rest)
    return dot(ones, high) + dot(ones, mid) + dot(ones, low)


def iota(shape, dim):
    return lax.broadcasted_iota(jnp.int32, shape, dim)


def near_order(n):
    return sorted(range(1, n), key=lambda k: (abs(k - n // 2), k))


def kernel(
    n, t, movie_hbm, traces_hbm, foot_hbm, block_hbm, neuron_hbm, fill_hbm,
    new_ref, grown_ref,
    movie, foot, block_ref, neuron_ref, fill_ref,
    all_traces, side_out, side_in, proj_out, proj_in, back_out, back_in,
    num_out, num_in, pow_out, pow_in,
    local_sem, send_sem, recv_sem, column_sem, side_send, side_recv, tm_send, tm_recv,
):
    me = lax.axis_index("pix")
    core = lax.axis_index("tm")
    slots = foot.shape[0]
    cap = slots // n
    neur = traces_hbm.shape[0]
    frames = movie.shape[1]
    blocks = movie.shape[0] // BLOCK
    neurons = n * neur
    wide = frames // PARTS
    pieces = range(PARTS)

    def wait_rest(ref, sem, rows, count=n - 1):
        rest = ref.at[pl.ds(0, count * rows)]
        pltpu.make_async_copy(rest, rest, sem).wait()

    def pix_id(peer):
        return (peer, core)

    def peers(body):
        if n <= 16:
            for k in near_order(n):
                body(lax.rem(me + k, n))
        else:
            lax.fori_loop(1, n, lambda k, _: (body(lax.rem(me + k, n)), 0)[1], 0)

    def part(index, size):
        return pl.ds(pl.multiple_of(index * size, size), size)

    barrier = pltpu.get_barrier_semaphore()
    peers(lambda p: pl.semaphore_signal(barrier, inc=1, device_id=pix_id(p)))
    for k in range(1, t):
        pl.semaphore_signal(barrier, inc=1, device_id=(me, lax.rem(core + k, t)))

    def mine(h):
        return all_traces.at[h, part(me, neur)]

    def strip(h):
        return slice(h * wide, (h + 1) * wide)

    loads = [
        pltpu.make_async_copy(a, b, local_sem.at[i])
        for i, (a, b) in enumerate(
            [(traces_hbm.at[:, pl.ds(h * wide, wide)], mine(h)) for h in pieces]
            + [
                (foot_hbm, foot),
                (block_hbm, block_ref),
                (neuron_hbm, neuron_ref),
                (fill_hbm, fill_ref),
                (movie_hbm, movie),
            ]
        )
    ]
    for load in loads:
        load.start()
    for h in pieces:
        loads[h].wait()
    pl.semaphore_wait(barrier, n - 1 + t - 1)

    planes = n // PLANE
    plane, spot = lax.div(me, PLANE), lax.rem(me, PLANE)

    def trace_copy(h, source, p, sem):
        return pltpu.make_async_remote_copy(
            src_ref=all_traces.at[h, part(source, neur)],
            dst_ref=all_traces.at[h, part(source, neur)],
            send_sem=send_sem.at[0, h],
            recv_sem=sem,
            device_id=pix_id(p),
        )

    def spread_plane(h, source):
        for k in range(1, PLANE):
            p = plane * PLANE + lax.rem(spot + k, PLANE)
            trace_copy(h, source, p, recv_sem.at[0, h]).start()

    def column_peer(k):
        return lax.rem(plane + k, planes) * PLANE + spot

    for h in pieces:
        for k in near_order(planes):
            trace_copy(h, me, column_peer(k), column_sem.at[h, k]).start()
        spread_plane(h, me)
    for load in loads[PARTS:-1]:
        load.wait()

    diag = iota((slots, slots), 0) == iota((slots, slots), 1)

    def column(row):
        return jnp.sum(jnp.where(diag, row.astype(F32), 0.0), axis=1, keepdims=True)

    block_row = block_ref[...].astype(F32)
    block_col = column(block_row)
    neuron_col = column(neuron_ref[...])
    owner_hit = lax.div(iota((slots, n), 0), cap) == iota((slots, n), 1)
    fill_col = jnp.sum(jnp.where(owner_hit, fill_ref[...].astype(F32), 0.0), axis=1, keepdims=True)
    row_of = iota((slots, 1), 0)
    usable = lax.rem(row_of, cap).astype(F32) < fill_col
    masked = jnp.where(usable, foot[...].astype(F32), 0.0)
    masked_b = masked.astype(BF16)
    same_block = block_col == block_row
    power = jnp.sum(masked * masked, axis=1, keepdims=True)
    lane = iota((slots, LANES), 1)
    place_of = lax.rem(row_of, cap)
    side = jnp.where(
        lane == place_of, neuron_col, jnp.where(lane == place_of + ROWS, power, 0.0)
    )
    to_owner = (lax.div(iota((n, slots), 1), cap) == iota((n, slots), 0)).astype(BF16)
    side = exact_dot(to_owner, side)
    for o in range(n):
        side_out[o] = side[o : o + 1, :]

    def side_copy(p, source):
        return pltpu.make_async_remote_copy(
            src_ref=side_out.at[p],
            dst_ref=side_in.at[source],
            send_sem=side_send.at[0],
            recv_sem=side_recv.at[0],
            device_id=pix_id(p),
        )

    peers(lambda p: side_copy(p, me).start())
    side_in[me] = side_out[me]

    padded = n * ROWS
    if cap == ROWS:
        widen = narrow = lambda x: x
    else:
        slot_row = lax.div(iota((padded, slots), 0), ROWS) * cap + lax.rem(
            iota((padded, slots), 0), ROWS
        )
        real = lax.rem(iota((padded, slots), 0), ROWS) < cap
        place = ((slot_row == iota((padded, slots), 1)) & real).astype(BF16)

        def widen(x):
            return dot(place, x).astype(BF16)

        def narrow(x):
            return dot(place, x, TN).astype(BF16)

    for h in pieces:
        for k in near_order(planes):
            source = column_peer(planes - k)
            trace_copy(h, source, source, column_sem.at[h, k]).wait_recv()
            spread_plane(h, source)

    gram = jnp.where(same_block, dot(masked_b, masked_b, NT), 0.0)
    neuron_id = lax.div(row_of, cap).astype(F32) * neur + neuron_col
    pick = (neuron_id == iota((slots, neurons), 1).astype(F32)).astype(BF16)
    gram_high, gram_low = split(gram)
    couple_high, couple_low = split(dot(gram_high, pick) + dot(gram_low, pick))

    loads[-1].wait()
    base = jnp.zeros((slots, frames), F32)
    for b in range(0, blocks, 2):
        pair = jnp.concatenate(
            [jnp.where(block_col == float(b + j), masked, 0.0).astype(BF16) for j in range(2)],
            axis=1,
        )
        base += dot(pair, movie[b * BLOCK : (b + 2) * BLOCK, :])

    def proj_copy(h, p, source):
        return pltpu.make_async_remote_copy(
            src_ref=proj_out.at[h, part(p, ROWS)],
            dst_ref=proj_in.at[h, part(source, ROWS)],
            send_sem=send_sem.at[1, h],
            recv_sem=recv_sem.at[1, h],
            device_id=pix_id(p),
        )

    for h in pieces:
        wait_rest(all_traces.at[h], recv_sem.at[0, h], neur, n - planes)
        gathered = all_traces[h]
        projection = base[:, strip(h)] - (dot(couple_high, gathered) + dot(couple_low, gathered))
        proj_out[h] = widen(projection.astype(BF16))
        peers(lambda p: proj_copy(h, p, me).start())
        proj_in[h, part(me, ROWS), :] = proj_out[h, part(me, ROWS), :]

    wait_rest(side_in, side_recv.at[0], 1)
    side_rows = jnp.concatenate([side_in[i] for i in range(n)], axis=0)
    from_tile = (lax.div(iota((padded, n), 0), ROWS) == iota((padded, n), 1)).astype(BF16)
    spread = exact_dot(from_tile, side_rows)
    spread_lane = iota((padded, LANES), 1)
    spread_place = lax.rem(iota((padded, 1), 0), ROWS)
    asked = jnp.sum(jnp.where(spread_lane == spread_place, spread, 0.0), axis=1, keepdims=True)
    asked_power = jnp.sum(
        jnp.where(spread_lane == spread_place + ROWS, spread, 0.0), axis=1, keepdims=True
    )
    hit = asked == iota((padded, neur), 1).astype(F32)
    if cap != ROWS:
        hit &= lax.rem(iota((padded, neur), 0), ROWS) < cap
    owner_pick = hit.astype(F32).astype(BF16)
    pick_turned = jnp.transpose(hit.astype(F32)).astype(BF16)
    total_power = exact_dot(pick_turned, jnp.broadcast_to(asked_power, (padded, LANES)))[:, 0:1]
    floor_power = jnp.maximum(total_power, 0.5)

    def back_copy(h, p, source):
        return pltpu.make_async_remote_copy(
            src_ref=back_out.at[h, part(p, ROWS)],
            dst_ref=back_in.at[h, part(source, ROWS)],
            send_sem=send_sem.at[2, h],
            recv_sem=recv_sem.at[2, h],
            device_id=pix_id(p),
        )

    for h in pieces:
        wait_rest(proj_in.at[h], recv_sem.at[1, h], ROWS)
        own = all_traces[h, part(me, neur), :].astype(F32)
        sums = dot(pick_turned, proj_in[h])
        updated = jnp.maximum(0.0, own + sums / floor_power).astype(BF16)
        back_out[h] = dot(owner_pick, updated).astype(BF16)
        peers(lambda p: back_copy(h, p, me).start())
        back_in[h, part(me, ROWS), :] = back_out[h, part(me, ROWS), :]
        new_ref[:, strip(h)] = updated

    for h in pieces:
        wait_rest(back_in.at[h], recv_sem.at[2, h], ROWS)
    fresh = jnp.concatenate([narrow(back_in[h]) for h in pieces], axis=1)
    fresh_f = fresh.astype(F32)
    pow_out[...] = jnp.broadcast_to(
        jnp.sum(fresh_f * fresh_f, axis=1, keepdims=True), (slots, BLOCK)
    )

    def tm_copy(index, out, into, q, source):
        return pltpu.make_async_remote_copy(
            src_ref=out,
            dst_ref=into.at[source],
            send_sem=tm_send.at[index, q],
            recv_sem=tm_recv.at[index, source],
            device_id=(me, q),
        )

    partners = [lax.rem(core + k, t) for k in range(1, t)]
    for q in partners:
        tm_copy(0, pow_out, pow_in, q, core).start()
    overlap = jnp.where(same_block, dot(fresh, fresh, NT), 0.0)
    over_high, over_low = split(overlap)
    numerator = -(dot(over_high, masked_b) + dot(over_low, masked_b))
    for b in range(0, blocks, 2):
        product = dot(fresh, movie[b * BLOCK : (b + 2) * BLOCK, :], NT)
        for j in range(2):
            numerator += jnp.where(
                block_col == float(b + j), product[:, j * BLOCK : (j + 1) * BLOCK], 0.0
            )
    num_out[...] = numerator
    for q in partners:
        tm_copy(1, num_out, num_in, q, core).start()
    pow_in[core] = pow_out[...]
    num_in[core] = numerator
    for q in partners:
        tm_copy(0, pow_out, pow_in, q, q).wait_recv()
        tm_copy(1, num_out, num_in, q, q).wait_recv()
    num_all, pow_all = num_in[0], pow_in[0]
    for q in range(1, t):
        num_all += num_in[q]
        pow_all += pow_in[q]
    grown = jnp.maximum(0.0, masked + num_all / (pow_all + 1e-06))
    grown_ref[...] = jnp.where(usable, grown, 0.0)

    wait_rest(side_out, side_send.at[0], 1)
    for h in pieces:
        wait_rest(all_traces.at[h], send_sem.at[0, h], neur)
        wait_rest(proj_out.at[h], send_sem.at[1, h], ROWS)
        wait_rest(back_out.at[h], send_sem.at[2, h], ROWS)
    for q in partners:
        tm_copy(0, pow_out, pow_in, q, core).wait_send()
        tm_copy(1, num_out, num_in, q, core).wait_send()


def settle(new_in, grown_in, new_out, grown_out):
    new_out[...] = new_in[...]
    grown_out[...] = grown_in[...]


def local(n, t, movie, traces, footprints, slot_block, slot_neuron, bucket_fill):
    slots = footprints.shape[0]
    neur, frames = traces.shape
    padded = n * ROWS
    wide = frames // PARTS
    results = (
        jax.ShapeDtypeStruct((neur, frames), BF16),
        jax.ShapeDtypeStruct((slots, BLOCK), F32),
    )
    swept = pl.pallas_call(
        functools.partial(kernel, n, t),
        out_shape=results,
        in_specs=[pl.BlockSpec(memory_space=pl.ANY)] * 6,
        out_specs=[pl.BlockSpec(memory_space=pltpu.VMEM)] * 2,
        scratch_shapes=[
            pltpu.VMEM(movie.shape, BF16),
            pltpu.VMEM(footprints.shape, BF16),
            pltpu.VMEM((1, slots), jnp.int32),
            pltpu.VMEM((1, slots), jnp.int32),
            pltpu.VMEM((1, n), jnp.int32),
            pltpu.VMEM((PARTS, n * neur, wide), BF16),
            pltpu.VMEM((n, 1, LANES), F32),
            pltpu.VMEM((n, 1, LANES), F32),
            pltpu.VMEM((PARTS, padded, wide), BF16),
            pltpu.VMEM((PARTS, padded, wide), BF16),
            pltpu.VMEM((PARTS, padded, wide), BF16),
            pltpu.VMEM((PARTS, padded, wide), BF16),
            pltpu.VMEM((slots, BLOCK), F32),
            pltpu.VMEM((t, slots, BLOCK), F32),
            pltpu.VMEM((slots, BLOCK), F32),
            pltpu.VMEM((t, slots, BLOCK), F32),
            pltpu.SemaphoreType.DMA((5 + PARTS,)),
            pltpu.SemaphoreType.DMA((3, PARTS)),
            pltpu.SemaphoreType.DMA((3, PARTS)),
            pltpu.SemaphoreType.DMA((PARTS, n // PLANE)),
            pltpu.SemaphoreType.DMA((1,)),
            pltpu.SemaphoreType.DMA((1,)),
            pltpu.SemaphoreType.DMA((2, t)),
            pltpu.SemaphoreType.DMA((2, t)),
        ],
        compiler_params=pltpu.CompilerParams(
            collective_id=0, has_side_effects=True, vmem_limit_bytes=VMEM_BYTES
        ),
    )(
        movie,
        traces,
        footprints,
        slot_block.reshape(1, slots),
        slot_neuron.reshape(1, slots),
        bucket_fill,
    )
    return pl.pallas_call(
        settle,
        out_shape=results,
        in_specs=[pl.BlockSpec(memory_space=pltpu.VMEM)] * 2,
        out_specs=[pl.BlockSpec(memory_space=pltpu.VMEM)] * 2,
        compiler_params=pltpu.CompilerParams(vmem_limit_bytes=VMEM_BYTES),
    )(*swept)


def solution(mesh):
    return jax.shard_map(
        functools.partial(local, mesh.shape["pix"], mesh.shape["tm"]),
        mesh=mesh,
        in_specs=(
            P("pix", "tm"),
            P("pix", "tm"),
            P("pix", None),
            P("pix"),
            P("pix"),
            P("pix", None),
        ),
        out_specs=(P("pix", "tm"), P("pix", None)),
        check_vma=False,
    )
```
